256 devices in a mesh: section: 16 (over x_lo, z), dp: 16 (over x_hi, y, core).
Axes of the slice: x: 4 (x_hi: 2, x_lo: 2; x = x_hi * 2 + x_lo), y: 4, z: 8, core: 2. Of those that a mesh axis runs over, the one named last changes fastest.
Arguments:
- w_value: bfloat16 [16, 2, 2304, 1024], P('section', None, 'dp'), as said below
- w_out_t: bfloat16 [16, 2, 2304, 1024], P('section', None, 'dp'), as said below
- layer_input: bfloat16 [16, 2, 2304, 2048], P('section', None, 'dp'), may hold values from -6 to 6
- grad_out: bfloat16 [16, 2, 2304, 2048], P('section', None, 'dp'), may hold values from -6 to 6
- heads_out: bfloat16 [16, 2048, 2, 1024], P('section', 'dp'), may hold values from -6 to 6
- probs: bfloat16 [16, 2, 8, 2048, 128], P('section', None, None, 'dp'), may hold values from 0 to 1, as said below
Outputs:
- next_down: bfloat16 [16, 2304, 2048], P('section', 'dp')
- next_up: bfloat16 [16, 2304, 2048], P('section', 'dp')
- grad_value: float32 [16, 2304, 1024], P('section', 'dp')
- grad_out_t: float32 [16, 2304, 1024], P('section', 'dp')
The draws below stay inside these ranges and needn't reach their ends.
Inputs may be any that keep to these rules, and one draw needn't show every extreme that they name: `w_value`: copy 1 of section s equals copy 0 of section 15 - s. `w_out_t`: copy 1 of section s equals copy 0 of section 15 - s. `probs`: within each sequence of 128 tokens a row is zero after the query's own position and sums to one up to bfloat16 rounding.
All inputs are finite; a program needn't handle non-finite values.
Results may differ from the reference program's by a relative error of at most 0.02.
Values may be sent and summed in bfloat16 or wider, within the bound.
A program may use at most 64 MiB of HBM per device.

```python
import jax
import jax.numpy as jnp
from jax import lax

D = 2304
HEADS = 8
HD = 128
SEQ = 128
HW = 1024
TOK = 2048
N_SECTION = 16
N_DP = 16


def weight_copies(seed_key, fan_in):
    base = jax.random.normal(seed_key, (N_SECTION, D, HW), jnp.float32) * (1.0 / fan_in) ** 0.5
    return jnp.stack([base, base[::-1]], axis=1).astype(jnp.bfloat16)


def draw_w_value(key, part):
    key = jax.random.fold_in(key, 11)
    return weight_copies(key, D)


def draw_w_out_t(key, part):
    key = jax.random.fold_in(key, 23)
    return weight_copies(key, HW)


def draw_probs(key, part):
    key = jax.random.fold_in(key, 37)
    logits = 1.5 * jax.random.normal(key, (N_SECTION, 2, HEADS, TOK, SEQ), jnp.float32)
    logits = jnp.clip(logits, -4.0, 4.0)
    query_pos = jnp.arange(TOK) % SEQ
    key_pos = jnp.arange(SEQ)
    allowed = key_pos[None, :] <= query_pos[:, None]
    unnormed = jnp.where(allowed, jnp.exp(logits), 0.0)
    return (unnormed / jnp.sum(unnormed, axis=-1, keepdims=True)).astype(jnp.bfloat16)


def spiked(drawn, own_key, source, target, blocks, factor):
    owner, partner = [(jnp.arange(drawn.shape[dim]) // (drawn.shape[dim] // blocks)).reshape([-1 if axis == dim else 1 for axis in range(drawn.ndim)]) for dim in (source, target)]
    chosen = jax.random.permutation(own_key, blocks)[partner]
    strong = (owner == chosen) | (owner == (partner + blocks // 2) % blocks)
    return jnp.where(strong, factor * drawn, drawn)


def shard_levels(own_key, dims, cuts, least, largest):
    def one(axis_at, shards_of):
        heights = jax.random.uniform(jax.random.fold_in(jax.random.fold_in(own_key, 6), axis_at), (shards_of,), jnp.float32, least / len(cuts), largest / len(cuts))
        return jnp.repeat(jnp.exp(heights), dims[axis_at] // shards_of).reshape((-1,) + (1,) * (len(dims) - axis_at - 1))

    level = one(*cuts[0])
    for cut in cuts[1:]:
        level = level * one(*cut)
    return level


def scatter_about(stream_key, extent, deviation, most, split=(), held_as=jnp.bfloat16):
    values = jax.random.normal(stream_key, extent, jnp.float32) * deviation
    if len(split) > 0:
        values = shard_levels(stream_key, extent, split, -0.22, 0.18) * values
    return jnp.clip(values, min=-most, max=most).astype(held_as)


def noise_with(key, dims, deviation, limit, shards, heavy, held_as=jnp.bfloat16):
    result = deviation * jax.random.normal(key, dims, jnp.float32)
    if shards:
        result = result * shard_levels(key, dims, shards, -0.22, 0.18)
    return jnp.clip(spiked(result, jax.random.fold_in(key, 3), *heavy), -limit, limit).astype(held_as)


def setup_inputs(seed: int = 0) -> dict:
    arg_keys = jax.random.split(jax.random.key(seed), 7)
    return {
        "w_value": draw_w_value(jax.random.fold_in(arg_keys[6], 71), 0),
        "w_out_t": draw_w_out_t(jax.random.fold_in(arg_keys[6], 71), 0),
        "layer_input": scatter_about(arg_keys[2], (N_SECTION, 2, D, TOK), 1.0, 6.0, ((0, 16), (2, 16))),
        "grad_out": noise_with(arg_keys[3], (N_SECTION, 2, D, TOK), 1.0, 6.0, ((0, 16), (2, 16)), (2, 3, 16, 2.0)),
        "heads_out": scatter_about(arg_keys[4], (N_SECTION, TOK, 2, HW), 1.0, 6.0, ((0, 16), (1, 16))),
        "probs": draw_probs(jax.random.fold_in(arg_keys[6], 71), 0),
    }


def section_copy(args):
    value_weight, out_weight, inputs, grads, heads, weights = args
    grad_blocks = grads.reshape(N_DP, D // N_DP, TOK).astype(jnp.float32)
    out_blocks = out_weight.reshape(N_DP, D // N_DP, HW).astype(jnp.float32)
    partial_terms = jnp.einsum("jft,jfh->jth", grad_blocks, out_blocks).astype(jnp.bfloat16)
    partial_terms = lax.optimization_barrier(partial_terms)
    head_sum = jnp.sum(partial_terms.astype(jnp.float32), axis=0)
    attn_grad = head_sum.astype(jnp.bfloat16).reshape(N_DP, SEQ, HEADS, HD)
    weight_blocks = weights.reshape(HEADS, N_DP, SEQ, SEQ)
    value_grad = jnp.einsum("hjqs,jqhe->jshe", weight_blocks.astype(jnp.float32), attn_grad.astype(jnp.float32))
    value_grad = value_grad.astype(jnp.bfloat16).reshape(TOK, HW)
    value_part = jnp.dot(inputs, value_grad, preferred_element_type=jnp.float32)
    out_part = jnp.dot(grads, heads, preferred_element_type=jnp.float32)
    backward = jnp.dot(value_weight, value_grad.T, preferred_element_type=jnp.float32)
    passed = (grads.astype(jnp.float32) + backward).astype(jnp.bfloat16)
    return value_part, out_part, passed


def reference(w_value, w_out_t, layer_input, grad_out, heads_out, probs):
    flat_heads = jnp.transpose(heads_out, (0, 2, 1, 3)).reshape(N_SECTION * 2, TOK, HW)
    inputs_all = (
        w_value.reshape(N_SECTION * 2, D, HW),
        w_out_t.reshape(N_SECTION * 2, D, HW),
        layer_input.reshape(N_SECTION * 2, D, TOK),
        grad_out.reshape(N_SECTION * 2, D, TOK),
        flat_heads,
        probs.reshape(N_SECTION * 2, HEADS, TOK, SEQ),
    )
    value_part, out_part, passed = lax.map(section_copy, inputs_all)
    value_part = value_part.reshape(N_SECTION, 2, D, HW)
    out_part = out_part.reshape(N_SECTION, 2, D, HW)
    passed = passed.reshape(N_SECTION, 2, D, TOK)
    empty = jnp.zeros((1, D, TOK), jnp.bfloat16)
    next_down = jnp.concatenate([passed[1:, 0], empty], axis=0)
    next_up = jnp.concatenate([empty, passed[:-1, 1]], axis=0)
    grad_value = value_part[:, 0] + value_part[::-1, 1]
    grad_out_t = out_part[:, 0] + out_part[::-1, 1]
    return next_down, next_up, grad_value, grad_out_t
```

```python
import itertools

import jax
import jax.numpy as jnp
from jax import lax
from jax.experimental import pallas as pl
from jax.experimental.pallas import tpu as pltpu
from jax.sharding import PartitionSpec as P

F = 144
T = 2048
H = 1024
SEQ = 128
HD = 128
HALF = 512
BF = jnp.bfloat16
F32 = jnp.float32
N_SEM = 112
N_LOCAL = 20


def contract(a, b, da, db):
    return lax.dot_general(a, b, (((da,), (db,)), ((), ())), preferred_element_type=F32)


def kernel(
    w_v, w_o, x_in, g_in, hd_in, pr_in,
    nxt, gval, gout,
    gall, goth, wall, hd, sp, own, r1, r2, pb, vall, xb, wvb, vacc, pacc, pbf,
    oacc, obk, orx, ofin, mo_s, mo_r, lo_r, mv_s, mv_r, lv_r, fin_o, fin_v, zero,
    ssem, rsem, lsem,
):
    sec = lax.axis_index("section")
    dp = lax.axis_index("dp")
    xh = dp // 8
    y = (dp // 2) % 4
    k = dp % 2
    o = 1 - k
    xo = 1 - xh
    yp, y2, ym = (y + 1) % 4, (y + 2) % 4, (y + 3) % 4
    around = (y, yp, y2, ym)

    def dev(a, b, c):
        return {"dp": a * 8 + b * 2 + c}

    sib, par, pao = dev(xh, y, o), dev(xo, y, k), dev(xo, y, o)
    up, dn = dev(xh, yp, k), dev(xh, ym, k)
    has_above = sec < 15
    has_below = sec > 0
    is0 = k == 0
    is1 = k == 1
    halo_ok = jnp.logical_or(jnp.logical_and(is0, has_below), jnp.logical_and(is1, has_above))
    halo_sec = jnp.clip(sec - 1 + 2 * k, 0, 15)

    counter = itertools.count()
    locals_ = itertools.count()
    sent = []

    def alloc(n=1):
        first = next(counter)
        for _ in range(n - 1):
            next(counter)
        assert first + n <= N_SEM
        return first

    def remote(src, dst, to, n, m=None):
        return pltpu.make_async_remote_copy(
            src_ref=src, dst_ref=dst, send_sem=ssem.at[n], recv_sem=rsem.at[n if m is None else m],
            device_id=to, device_id_type=pl.DeviceIdType.MESH,
        )

    def push(src, dst, to, n=None):
        copy = remote(src, dst, to, alloc() if n is None else n)
        copy.start()
        sent.append(copy)
        return copy

    def arrive(dst, n):
        remote(dst, dst, sib, n).wait_recv()

    def pull(src, dst):
        copy = pltpu.make_async_copy(src, dst, lsem.at[next(locals_)])
        copy.start()
        return copy

    tcol = xh * 1024
    ocol = xo * 1024

    def cols(base, yy, width=256):
        return pl.ds(pl.multiple_of(base + yy * 256, 256), width)

    own_w = pull(w_o.at[k], wall.at[k])
    own_g = [pull(g_in.at[k, :, cols(tcol, yy)], gall.at[yy, k]) for yy in range(4)]
    own_hd = pull(hd_in.at[k], hd.at[y, k])
    own_rest = [
        pull(pr_in.at[k], pb.at[k]),
        pull(w_v.at[k], wvb.at[k]),
        pull(x_in.at[k], xb.at[k]),
        pull(g_in.at[k, :, cols(ocol, 0, 1024)], goth.at[k]),
    ]

    barrier = pltpu.get_barrier_semaphore()

    def greet(to):
        pl.semaphore_signal(barrier, inc=1, device_id=to, device_id_type=pl.DeviceIdType.MESH)

    for to in (sib, par, pao, up, dn):
        greet(to)
    greet({"section": 15 - sec, "dp": xh * 8 + y * 2 + 1})

    @pl.when(has_above)
    def _():
        greet({"section": jnp.minimum(sec + 1, 15), "dp": xh * 8 + y * 2})

    @pl.when(has_below)
    def _():
        greet({"section": jnp.maximum(sec - 1, 0), "dp": xh * 8 + y * 2 + 1})

    pl.semaphore_wait(barrier, 5 + 2 * k + 2 * halo_ok.astype(jnp.int32))

    h_up, h_dn = alloc(2), alloc(2)
    hd_sib = push(hd_in.at[o], hd.at[y, k], sib)
    push(hd_in.at[k], hd.at[y, k], up, h_up + k)
    push(hd_in.at[k], hd.at[y, k], dn, h_dn + k)
    w_copies = [
        push(w_o.at[o], wall.at[k], sib),
        push(w_o.at[k], wall.at[2 + k], par),
        push(w_o.at[o], wall.at[2 + k], pao),
    ]
    g_copies = {}
    for d in (2, 1, 3, 0):
        yy = around[d]
        g_copies[d] = [
            push(g_in.at[o, :, cols(tcol, yy)], gall.at[yy, k], sib),
            push(g_in.at[k, :, cols(ocol, yy)], gall.at[yy, 2 + k], par),
            push(g_in.at[o, :, cols(ocol, yy)], gall.at[yy, 2 + k], pao),
        ]

    hd_sib.wait_recv()
    push(hd.at[y, o], hd.at[y, o], up, h_up + o)
    push(hd.at[y, o], hd.at[y, o], dn, h_dn + o)
    rest = [
        push(pr_in.at[o], pb.at[k], sib),
        push(w_v.at[o], wvb.at[k], sib),
        push(x_in.at[o], xb.at[k], sib),
        push(g_in.at[o, :, cols(ocol, 0, 1024)], goth.at[k], sib),
    ]

    zero[...] = jnp.zeros_like(zero)
    edge = jnp.where(has_above, 1, 0)
    no_edge = jnp.logical_and(has_above, has_below)
    zero_copy = pltpu.make_async_copy(zero, nxt.at[edge], lsem.at[next(locals_)])

    @pl.when(jnp.logical_not(no_edge))
    def _():
        zero_copy.start()

    arrive(hd.at[ym, 0], h_up)
    hd_f_up = push(hd.at[ym, 0], hd.at[ym, 0], up)
    arrive(hd.at[yp, 1], h_dn + 1)
    hd_f_dn = push(hd.at[yp, 1], hd.at[yp, 1], dn)

    own_w.wait()
    for copy in own_g:
        copy.wait()
    for copy in w_copies:
        copy.wait_recv()

    def partial(d):
        for copy in g_copies[d]:
            copy.wait_recv()
        part = contract(
            gall[around[d]].reshape(4 * F, 256), wall[...].reshape(4 * F, H), 0, 0
        )
        for h in range(2):
            for q in range(2):
                piece = part[q * SEQ : (q + 1) * SEQ, h * HALF : (h + 1) * HALF]
                if d == 0:
                    own[h, q] = piece
                else:
                    sp[d, h, q] = piece.astype(BF)

    def out_term(d, first=False):
        term = contract(
            gall[around[d]].reshape(4 * F, 256), hd[around[d]].reshape(256, H), 1, 0
        )
        if first:
            oacc[...] = term
        else:
            oacc[...] += term

    s1 = {}
    s2 = {}

    def ring_first(h):
        s1[h] = [
            push(sp.at[2, h, 0], r1.at[0, h], up),
            push(sp.at[2, h, 1], r1.at[1, h], dn),
        ]

    def ring_up(h):
        s2[h, 0] = push(sp.at[1, h, 1], r2.at[0, h, 1], up)

    def ring_dn(h):
        s2[h, 1] = push(sp.at[3, h, 0], r2.at[1, h, 0], dn)

    def ring_sum(h):
        s1[h][0].wait_recv()
        sp[1, h, 0] = (sp[1, h, 0].astype(F32) + r1[0, h].astype(F32)).astype(BF)
        s2[h, 2] = push(sp.at[1, h, 0], r2.at[0, h, 0], up)
        s1[h][1].wait_recv()
        sp[3, h, 1] = (sp[3, h, 1].astype(F32) + r1[1, h].astype(F32)).astype(BF)
        s2[h, 3] = push(sp.at[3, h, 1], r2.at[1, h, 1], dn)

    partial(2)
    ring_first(0)
    partial(1)
    ring_up(0)
    own_hd.wait()
    arrive(hd.at[yp, 0], h_dn)
    out_term(1, first=True)
    partial(3)
    ring_dn(0)
    arrive(hd.at[ym, 1], h_up + 1)
    out_term(3)
    ring_sum(0)
    ring_first(1)
    ring_up(1)
    ring_dn(1)
    partial(0)
    out_term(0)
    hd_f_up.wait_recv()
    hd_f_dn.wait_recv()
    out_term(2)
    obk[...] = oacc[2 * F :].astype(BF).reshape(2, F, H)

    for copy in own_rest:
        copy.wait()
    for copy in rest:
        copy.wait_recv()

    v_sent = {}

    def attention(h):
        for i in range(4):
            s2[h, i].wait_recv()
        for q in range(2):
            total = own[h, q] + r2[0, h, q].astype(F32) + r2[1, h, q].astype(F32)
            total = total.astype(BF)
            for e in range(4):
                vall[h, xh, y, q, :, e * HD : (e + 1) * HD] = contract(
                    pb[q, h * 4 + e], total[:, e * HD : (e + 1) * HD], 0, 0
                ).astype(BF)
        mine = vall.at[h, xh, y]
        v_sent[h, "x"] = push(mine, mine, par)
        v_sent[h, 0, "u"] = push(mine, mine, up)
        v_sent[h, 0, "d"] = push(mine, mine, dn)

    def spread_other(h):
        v_sent[h, "x"].wait_recv()
        other = vall.at[h, xo, y]
        v_sent[h, 1, "u"] = push(other, other, up)
        v_sent[h, 1, "d"] = push(other, other, dn)

    def forward(h, side):
        xx = (xh, xo)[side]
        v_sent[h, side, "u"].wait_recv()
        piece = vall.at[h, xx, ym, 0]
        v_sent[h, side, "fu"] = push(piece, piece, up)
        v_sent[h, side, "d"].wait_recv()
        piece = vall.at[h, xx, yp, 1]
        v_sent[h, side, "fd"] = push(piece, piece, dn)

    def far(h, side):
        v_sent[h, side, "fu"].wait_recv()
        v_sent[h, side, "fd"].wait_recv()

    halo_sem = alloc(16)
    halo_send = alloc(16)
    halos = []

    def use(h, side, d, first=False):
        xx, yy = (xh, xo)[side], around[d]
        at = cols(xx * 1024, yy)
        block = vall[h, xx, yy].reshape(256, HALF)
        term = contract(xb[:, :, at].reshape(2 * F, 256), block, 1, 0).reshape(2, F, HALF)
        if first:
            vacc[h] = term
        else:
            vacc[h] += term
        back = contract(
            wvb[:, :, h * HALF : (h + 1) * HALF].reshape(2 * F, HALF), block, 1, 1
        )
        i = side * 4 + d
        if h == 0:
            pacc[i] = back
            return
        g_here = gall[yy, 0:2] if side == 0 else goth[:, :, cols(0, yy)]
        total = g_here.reshape(2 * F, 256).astype(F32) + (pacc[i] + back)
        pbf[i] = total.astype(BF).reshape(2, F, 256)
        copies = [
            remote(
                pbf.at[i, b], nxt.at[k, :, at],
                {"section": halo_sec, "dp": xh * 8 + y * 2 + b},
                halo_send + 2 * i + b, halo_sem + 8 * k + i,
            )
            for b in range(2)
        ]
        halos.extend(copies)

        @pl.when(halo_ok)
        def _():
            for copy in copies:
                copy.start()

    mirror = [{"section": 15 - sec, "dp": xh * 8 + y * 2 + b} for b in range(2)]
    m_out, m_val = alloc(2), [alloc(2), alloc(2)]
    l_out, l_val = alloc(), [alloc(), alloc()]
    mirrors = []
    handed = []

    def share(result, send, land, land_core, n_mirror, n_core):
        copies = [remote(send.at[b], land, mirror[b], n_mirror + b, n_mirror) for b in range(2)]
        mirrors.extend(copies)
        over = remote(result.at[1], land_core, sib, n_core)
        handed.append(over)

        @pl.when(is1)
        def _():
            send[...] = result[...].astype(BF)
            for copy in copies:
                copy.start()

        @pl.when(is0)
        def _():
            over.start()

    stores = []

    def settle(result, land, land_core, n_mirror, n_core, total, target):
        @pl.when(is0)
        def _():
            land_core[...] = result[0]

        @pl.when(is1)
        def _():
            arrive(land_core, n_core)

        arrive(land, n_mirror)
        total[...] = land_core[...] + land[...].astype(F32)
        stores.append(pull(total, target))

    def settle_value(h):
        settle(
            vacc.at[h], mv_r.at[h], lv_r.at[h], m_val[h], l_val[h],
            fin_v.at[h], gval.at[:, pl.ds(h * HALF, HALF)],
        )

    attention(0)
    out_back = push(obk, orx, par)
    ring_sum(1)
    use(0, 0, 0, first=True)
    spread_other(0)
    forward(0, 0)
    attention(1)
    use(0, 1, 0)
    use(0, 0, 1)
    use(0, 0, 3)
    forward(0, 1)
    spread_other(1)
    use(1, 0, 0, first=True)
    use(0, 1, 1)
    use(0, 1, 3)
    far(0, 0)
    use(0, 0, 2)
    use(1, 1, 0)
    forward(1, 0)
    out_back.wait_recv()
    ofin[...] = oacc[: 2 * F].reshape(2, F, H) + orx[...].astype(F32)
    share(ofin, mo_s, mo_r, lo_r, m_out, l_out)
    far(0, 1)
    use(0, 1, 2)
    share(vacc.at[0], mv_s.at[0], mv_r.at[0], lv_r.at[0], m_val[0], l_val[0])
    use(1, 0, 1)
    use(1, 0, 3)
    forward(1, 1)
    use(1, 1, 1)
    use(1, 1, 3)
    settle(ofin, mo_r, lo_r, m_out, l_out, fin_o, gout)
    far(1, 0)
    use(1, 0, 2)
    settle_value(0)
    far(1, 1)
    use(1, 1, 2)
    share(vacc.at[1], mv_s.at[1], mv_r.at[1], lv_r.at[1], m_val[1], l_val[1])

    for copy in sent:
        copy.wait_send()

    @pl.when(halo_ok)
    def _():
        for copy in halos:
            copy.wait_send()

    @pl.when(jnp.logical_not(no_edge))
    def _():
        zero_copy.wait()

    for core, there in ((0, has_above), (1, has_below)):

        @pl.when(there)
        def _(core=core):
            for i in range(8):
                arrive(nxt.at[core, :, pl.ds(i * 256, 256)], halo_sem + 8 * core + i)

    settle_value(1)

    @pl.when(is1)
    def _():
        for copy in mirrors:
            copy.wait_send()

    @pl.when(is0)
    def _():
        for copy in handed:
            copy.wait_send()

    for copy in stores:
        copy.wait()


def on_device(w_value, w_out_t, layer_input, grad_out, heads_out, probs):
    heads = jnp.swapaxes(heads_out[0], 0, 1)
    any_ = pl.BlockSpec(memory_space=pl.ANY)
    scratch = [
        ((4, 4, F, 256), BF),
        ((2, F, 1024), BF),
        ((4, F, H), BF),
        ((4, 2, SEQ, H), BF),
        ((4, 2, 2, SEQ, HALF), BF),
        ((2, 2, SEQ, HALF), F32),
        ((2, 2, SEQ, HALF), BF),
        ((2, 2, 2, SEQ, HALF), BF),
        ((2, 8, SEQ, SEQ), BF),
        ((2, 2, 4, 2, SEQ, HALF), BF),
        ((2, F, T), BF),
        ((2, F, H), BF),
        ((2, 2, F, HALF), F32),
        ((8, 2 * F, 256), F32),
        ((8, 2, F, 256), BF),
        ((4 * F, H), F32),
        ((2, F, H), BF),
        ((2, F, H), BF),
        ((2, F, H), F32),
        ((2, F, H), BF),
        ((F, H), BF),
        ((F, H), F32),
        ((2, 2, F, HALF), BF),
        ((2, F, HALF), BF),
        ((2, F, HALF), F32),
        ((F, H), F32),
        ((2, F, HALF), F32),
        ((F, T), BF),
    ]
    nxt, gval, gout = pl.pallas_call(
        kernel,
        out_shape=(
            jax.ShapeDtypeStruct((2, F, T), BF),
            jax.ShapeDtypeStruct((F, H), F32),
            jax.ShapeDtypeStruct((F, H), F32),
        ),
        in_specs=[any_] * 6,
        out_specs=(any_, any_, any_),
        scratch_shapes=[pltpu.VMEM(shape, dtype) for shape, dtype in scratch]
        + [
            pltpu.SemaphoreType.DMA((N_SEM,)),
            pltpu.SemaphoreType.DMA((N_SEM,)),
            pltpu.SemaphoreType.DMA((N_LOCAL,)),
        ],
        compiler_params=pltpu.CompilerParams(
            collective_id=0, has_side_effects=True, vmem_limit_bytes=52 * 2**20
        ),
        cost_estimate=pl.CostEstimate(
            flops=5_000_000_000, bytes_accessed=8_000_000, transcendentals=0
        ),
    )(w_value[0], w_out_t[0], layer_input[0], grad_out[0], heads, probs[0])
    return nxt[0][None], nxt[1][None], gval[None], gout[None]


def solution(mesh):
    in_specs = (
        P("section", None, "dp", None),
        P("section", None, "dp", None),
        P("section", None, "dp", None),
        P("section", None, "dp", None),
        P("section", "dp", None, None),
        P("section", None, None, "dp", None),
    )
    out_specs = (P("section", "dp", None),) * 4
    return jax.shard_map(
        on_device, mesh=mesh, in_specs=in_specs, out_specs=out_specs, check_vma=False
    )
```

```python
import itertools

import jax
import jax.numpy as jnp
from jax import lax
from jax.experimental import pallas as pl
from jax.experimental.pallas import tpu as pltpu
from jax.sharding import PartitionSpec as P

F = 144
T = 2048
H = 1024
SEQ = 128
HD = 128
HALF = 512
BF = jnp.bfloat16
F32 = jnp.float32
N_SEM = 112
N_LOCAL = 20


def contract(a, b, da, db):
    return lax.dot_general(a, b, (((da,), (db,)), ((), ())), preferred_element_type=F32)


def kernel(
    w_v, w_o, x_in, g_in, hd_in, pr_in,
    ndn, nup, gval, gout,
    raw, hc, gall, goth, wall, hd, sp, own, r1, r2, pb, vall, xb, wvb, vacc, pacc, pbf,
    oacc, obk, orx, ofin, mo_s, mo_r, lo_r, mv_s, mv_r, lv_r, fin_o, fin_v, zero,
    ssem, rsem, lsem,
):
    sec = lax.axis_index("section")
    dp = lax.axis_index("dp")
    xh = dp // 8
    y = (dp // 2) % 4
    k = dp % 2
    o = 1 - k
    xo = 1 - xh
    yp, y2, ym = (y + 1) % 4, (y + 2) % 4, (y + 3) % 4
    around = (y, yp, y2, ym)

    def dev(a, b, c):
        return {"dp": a * 8 + b * 2 + c}

    sib, par, pao = dev(xh, y, o), dev(xo, y, k), dev(xo, y, o)
    up, dn = dev(xh, yp, k), dev(xh, ym, k)
    has_above = sec < 15
    has_below = sec > 0
    is0 = k == 0
    is1 = k == 1
    halo_ok = jnp.logical_or(jnp.logical_and(is0, has_below), jnp.logical_and(is1, has_above))
    halo_sec = jnp.clip(sec - 1 + 2 * k, 0, 15)

    counter = itertools.count()
    locals_ = itertools.count()
    sent = []

    def alloc(n=1):
        first = next(counter)
        for _ in range(n - 1):
            next(counter)
        assert first + n <= N_SEM
        return first

    def remote(src, dst, to, n, m=None):
        return pltpu.make_async_remote_copy(
            src_ref=src, dst_ref=dst, send_sem=ssem.at[n], recv_sem=rsem.at[n if m is None else m],
            device_id=to, device_id_type=pl.DeviceIdType.MESH,
        )

    def push(src, dst, to, n=None):
        copy = remote(src, dst, to, alloc() if n is None else n)
        copy.start()
        sent.append(copy)
        return copy

    def arrive(dst, n):
        remote(dst, dst, sib, n).wait_recv()

    def pull(src, dst):
        copy = pltpu.make_async_copy(src, dst, lsem.at[next(locals_)])
        copy.start()
        return copy

    tcol = xh * 1024
    ocol = xo * 1024

    def cols(base, yy, width=256):
        return pl.ds(pl.multiple_of(base + yy * 256, 256), width)

    own_hd = pull(hd_in, raw)
    own_w = pull(w_o.at[k], wall.at[k])
    own_g = [pull(g_in.at[k, :, cols(tcol, yy)], gall.at[yy, k]) for yy in range(4)]
    own_rest = [
        pull(pr_in.at[k], pb.at[k]),
        pull(w_v.at[k], wvb.at[k]),
        pull(x_in.at[k], xb.at[k]),
        pull(g_in.at[k, :, cols(ocol, 0, 1024)], goth.at[k]),
    ]

    barrier = pltpu.get_barrier_semaphore()

    def greet(to):
        pl.semaphore_signal(barrier, inc=1, device_id=to, device_id_type=pl.DeviceIdType.MESH)

    for to in (sib, par, pao, up, dn):
        greet(to)
    greet({"section": 15 - sec, "dp": xh * 8 + y * 2 + 1})

    @pl.when(has_above)
    def _():
        greet({"section": jnp.minimum(sec + 1, 15), "dp": xh * 8 + y * 2})

    @pl.when(has_below)
    def _():
        greet({"section": jnp.maximum(sec - 1, 0), "dp": xh * 8 + y * 2 + 1})

    own_hd.wait()
    for c in range(2):
        hc[c] = raw[:, c, :]
    hd[y, k] = hc[k]
    pl.semaphore_wait(barrier, 5 + 2 * k + 2 * halo_ok.astype(jnp.int32))

    h_up, h_dn = alloc(2), alloc(2)
    hd_sib = push(hc.at[o], hd.at[y, k], sib)
    push(hc.at[k], hd.at[y, k], up, h_up + k)
    push(hc.at[k], hd.at[y, k], dn, h_dn + k)
    w_copies = [
        push(w_o.at[o], wall.at[k], sib),
        push(w_o.at[k], wall.at[2 + k], par),
        push(w_o.at[o], wall.at[2 + k], pao),
    ]
    g_copies = {}

    def send_g(d):
        yy = around[d]
        g_copies[d] = [
            push(g_in.at[o, :, cols(tcol, yy)], gall.at[yy, k], sib),
            push(g_in.at[k, :, cols(ocol, yy)], gall.at[yy, 2 + k], par),
            push(g_in.at[o, :, cols(ocol, yy)], gall.at[yy, 2 + k], pao),
        ]

    for d in (2, 1, 3, 0):
        send_g(d)

    hd_sib.wait_recv()
    push(hd.at[y, o], hd.at[y, o], up, h_up + o)
    push(hd.at[y, o], hd.at[y, o], dn, h_dn + o)
    rest = [
        push(pr_in.at[o], pb.at[k], sib),
        push(w_v.at[o], wvb.at[k], sib),
        push(x_in.at[o], xb.at[k], sib),
        push(g_in.at[o, :, cols(ocol, 0, 1024)], goth.at[k], sib),
    ]

    zero[...] = jnp.zeros_like(zero)
    zero_sem = next(locals_)

    @pl.when(jnp.logical_not(has_above))
    def _():
        pltpu.make_async_copy(zero, ndn, lsem.at[zero_sem]).start()

    @pl.when(jnp.logical_not(has_below))
    def _():
        pltpu.make_async_copy(zero, nup, lsem.at[zero_sem]).start()

    arrive(hd.at[ym, 0], h_up)
    hd_f_up = push(hd.at[ym, 0], hd.at[ym, 0], up)
    arrive(hd.at[yp, 1], h_dn + 1)
    hd_f_dn = push(hd.at[yp, 1], hd.at[yp, 1], dn)

    own_w.wait()
    for copy in own_g:
        copy.wait()
    for copy in w_copies:
        copy.wait_recv()

    def partial(d):
        for copy in g_copies[d]:
            copy.wait_recv()
        part = contract(
            gall[around[d]].reshape(4 * F, 256), wall[...].reshape(4 * F, H), 0, 0
        )
        for h in range(2):
            for q in range(2):
                piece = part[q * SEQ : (q + 1) * SEQ, h * HALF : (h + 1) * HALF]
                if d == 0:
                    own[h, q] = piece
                else:
                    sp[d, h, q] = piece.astype(BF)

    def out_term(d, first=False):
        term = contract(
            gall[around[d]].reshape(4 * F, 256), hd[around[d]].reshape(256, H), 1, 0
        )
        for h in range(2):
            half = term[:, h * HALF : (h + 1) * HALF].reshape(4, F, HALF)
            if first:
                oacc[h] = half
            else:
                oacc[h] += half

    s1 = {}
    s2 = {}

    def ring_first(h):
        s1[h] = [
            push(sp.at[2, h, 0], r1.at[0, h], up),
            push(sp.at[2, h, 1], r1.at[1, h], dn),
        ]

    def ring_up(h):
        s2[h, 0] = push(sp.at[1, h, 1], r2.at[0, h, 1], up)

    def ring_dn(h):
        s2[h, 1] = push(sp.at[3, h, 0], r2.at[1, h, 0], dn)

    def ring_sum(h):
        s1[h][0].wait_recv()
        sp[1, h, 0] = (sp[1, h, 0].astype(F32) + r1[0, h].astype(F32)).astype(BF)
        s2[h, 2] = push(sp.at[1, h, 0], r2.at[0, h, 0], up)
        s1[h][1].wait_recv()
        sp[3, h, 1] = (sp[3, h, 1].astype(F32) + r1[1, h].astype(F32)).astype(BF)
        s2[h, 3] = push(sp.at[3, h, 1], r2.at[1, h, 1], dn)

    partial(2)
    ring_first(0)
    ring_first(1)
    partial(1)
    ring_up(0)
    arrive(hd.at[yp, 0], h_dn)
    out_term(1, first=True)
    partial(3)
    ring_dn(0)
    ring_sum(0)
    ring_up(1)
    ring_dn(1)
    ring_sum(1)
    arrive(hd.at[ym, 1], h_up + 1)
    out_term(3)
    hd_f_up.wait_recv()
    hd_f_dn.wait_recv()
    out_term(2)
    partial(0)
    out_term(0)
    for h in range(2):
        obk[h] = oacc[h, 2:4].astype(BF)
    out_back = [push(obk.at[0], orx.at[0], par)]

    for copy in own_rest:
        copy.wait()
    for copy in rest:
        copy.wait_recv()

    v_sent = {}

    def attention(h):
        for i in range(4):
            s2[h, i].wait_recv()
        for q in range(2):
            total = own[h, q] + r2[0, h, q].astype(F32) + r2[1, h, q].astype(F32)
            total = total.astype(BF)
            for e in range(4):
                vall[h, xh, y, q, :, e * HD : (e + 1) * HD] = contract(
                    pb[q, h * 4 + e], total[:, e * HD : (e + 1) * HD], 0, 0
                ).astype(BF)
        mine = vall.at[h, xh, y]
        v_sent[h, "x"] = push(mine, mine, par)

    def spread_own(h):
        mine = vall.at[h, xh, y]
        v_sent[h, 0, "u"] = push(mine, mine, up)
        v_sent[h, 0, "d"] = push(mine, mine, dn)

    def spread_other(h):
        v_sent[h, "x"].wait_recv()
        other = vall.at[h, xo, y]
        v_sent[h, 1, "u"] = push(other, other, up)
        v_sent[h, 1, "d"] = push(other, other, dn)

    def forward(h, side):
        xx = (xh, xo)[side]
        v_sent[h, side, "u"].wait_recv()
        piece = vall.at[h, xx, ym, 0]
        v_sent[h, side, "fu"] = push(piece, piece, up)
        v_sent[h, side, "d"].wait_recv()
        piece = vall.at[h, xx, yp, 1]
        v_sent[h, side, "fd"] = push(piece, piece, dn)

    def far(h, side):
        v_sent[h, side, "fu"].wait_recv()
        v_sent[h, side, "fd"].wait_recv()

    halo_sem = alloc(16)
    halo_send = alloc(16)
    halos = []

    def use(h, side, d, first=False):
        xx, yy = (xh, xo)[side], around[d]
        at = cols(xx * 1024, yy)
        block = vall[h, xx, yy].reshape(256, HALF)
        term = contract(xb[:, :, at].reshape(2 * F, 256), block, 1, 0).reshape(2, F, HALF)
        if first:
            vacc[h] = term
        else:
            vacc[h] += term
        back = contract(
            wvb[:, :, h * HALF : (h + 1) * HALF].reshape(2 * F, HALF), block, 1, 1
        )
        i = side * 4 + d
        if h == 0:
            pacc[i] = back
            return
        g_here = gall[yy, 0:2] if side == 0 else goth[:, :, cols(0, yy)]
        total = g_here.reshape(2 * F, 256).astype(F32) + (pacc[i] + back)
        pbf[i] = total.astype(BF).reshape(2, F, 256)
        for core, there, out in ((is0, has_below, ndn), (is1, has_above, nup)):
            copies = [
                remote(
                    pbf.at[i, b], out.at[:, at],
                    {"section": halo_sec, "dp": xh * 8 + y * 2 + b},
                    halo_send + 2 * i + b, halo_sem + 8 * k + i,
                )
                for b in range(2)
            ]

            @pl.when(jnp.logical_and(core, there))
            def _(copies=copies):
                for copy in copies:
                    copy.start()

        halos.extend(copies)

    mirror = [{"section": 15 - sec, "dp": xh * 8 + y * 2 + b} for b in range(2)]
    m_out, m_val = [alloc(2), alloc(2)], [alloc(2), alloc(2)]
    l_out, l_val = [alloc(), alloc()], [alloc(), alloc()]
    mirrors = []
    handed = []

    def share(result, send, land, land_core, n_mirror, n_core):
        copies = [remote(send.at[b], land, mirror[b], n_mirror + b, n_mirror) for b in range(2)]
        mirrors.extend(copies)
        over = remote(result.at[1], land_core, sib, n_core)
        handed.append(over)

        @pl.when(is1)
        def _():
            send[...] = result[...].astype(BF)
            for copy in copies:
                copy.start()

        @pl.when(is0)
        def _():
            over.start()

    stores = []

    def settle(result, land, land_core, n_mirror, n_core, total, target):
        @pl.when(is0)
        def _():
            land_core[...] = result[0]

        @pl.when(is1)
        def _():
            arrive(land_core, n_core)

        arrive(land, n_mirror)
        total[...] = land_core[...] + land[...].astype(F32)
        stores.append(pull(total, target))

    def share_out(h):
        out_back[h].wait_recv()
        ofin[h] = oacc[h, 0:2] + orx[h].astype(F32)
        share(ofin.at[h], mo_s.at[h], mo_r.at[h], lo_r.at[h], m_out[h], l_out[h])

    def share_value(h):
        share(vacc.at[h], mv_s.at[h], mv_r.at[h], lv_r.at[h], m_val[h], l_val[h])

    def settle_out(h):
        settle(
            ofin.at[h], mo_r.at[h], lo_r.at[h], m_out[h], l_out[h],
            fin_o.at[h], gout.at[:, pl.ds(h * HALF, HALF)],
        )

    def settle_value(h):
        settle(
            vacc.at[h], mv_r.at[h], lv_r.at[h], m_val[h], l_val[h],
            fin_v.at[h], gval.at[:, pl.ds(h * HALF, HALF)],
        )

    attention(0)
    spread_own(0)
    out_back.append(push(obk.at[1], orx.at[1], par))
    attention(1)
    spread_other(0)
    use(0, 0, 0, first=True)
    share_out(0)
    use(1, 0, 0, first=True)
    forward(0, 0)
    use(0, 1, 0)
    share_out(1)
    use(0, 0, 1)
    use(0, 0, 3)
    forward(0, 1)
    spread_own(1)
    spread_other(1)
    use(1, 1, 0)
    use(0, 1, 1)
    use(0, 1, 3)
    far(0, 0)
    use(0, 0, 2)
    far(0, 1)
    use(0, 1, 2)
    share_value(0)
    forward(1, 0)
    use(1, 0, 1)
    use(1, 0, 3)
    settle_out(0)
    forward(1, 1)
    use(1, 1, 1)
    use(1, 1, 3)
    settle_out(1)
    far(1, 0)
    use(1, 0, 2)
    far(1, 1)
    use(1, 1, 2)
    share_value(1)
    settle_value(0)

    for copy in sent:
        copy.wait_send()

    @pl.when(halo_ok)
    def _():
        for copy in halos:
            copy.wait_send()

    @pl.when(jnp.logical_not(jnp.logical_and(has_above, has_below)))
    def _():
        pltpu.make_async_copy(zero, ndn, lsem.at[zero_sem]).wait()

    for core, there, out in ((0, has_above, ndn), (1, has_below, nup)):

        @pl.when(there)
        def _(core=core, out=out):
            for i in range(8):
                arrive(out.at[:, pl.ds(i * 256, 256)], halo_sem + 8 * core + i)

    settle_value(1)

    @pl.when(is1)
    def _():
        for copy in mirrors:
            copy.wait_send()

    @pl.when(is0)
    def _():
        for copy in handed:
            copy.wait_send()

    for copy in stores:
        copy.wait()


def on_device(w_value, w_out_t, layer_input, grad_out, heads_out, probs):
    any_ = pl.BlockSpec(memory_space=pl.ANY)
    scratch = [
        ((SEQ, 2, H), BF),
        ((2, SEQ, H), BF),
        ((4, 4, F, 256), BF),
        ((2, F, 1024), BF),
        ((4, F, H), BF),
        ((4, 2, SEQ, H), BF),
        ((4, 2, 2, SEQ, HALF), BF),
        ((2, 2, SEQ, HALF), F32),
        ((2, 2, SEQ, HALF), BF),
        ((2, 2, 2, SEQ, HALF), BF),
        ((2, 8, SEQ, SEQ), BF),
        ((2, 2, 4, 2, SEQ, HALF), BF),
        ((2, F, T), BF),
        ((2, F, H), BF),
        ((2, 2, F, HALF), F32),
        ((8, 2 * F, 256), F32),
        ((8, 2, F, 256), BF),
        ((2, 4, F, HALF), F32),
        ((2, 2, F, HALF), BF),
        ((2, 2, F, HALF), BF),
        ((2, 2, F, HALF), F32),
        ((2, 2, F, HALF), BF),
        ((2, F, HALF), BF),
        ((2, F, HALF), F32),
        ((2, 2, F, HALF), BF),
        ((2, F, HALF), BF),
        ((2, F, HALF), F32),
        ((2, F, HALF), F32),
        ((2, F, HALF), F32),
        ((F, T), BF),
    ]
    down, above, gval, gout = pl.pallas_call(
        kernel,
        out_shape=(
            jax.ShapeDtypeStruct((F, T), BF),
            jax.ShapeDtypeStruct((F, T), BF),
            jax.ShapeDtypeStruct((F, H), F32),
            jax.ShapeDtypeStruct((F, H), F32),
        ),
        in_specs=[any_] * 6,
        out_specs=(any_,) * 4,
        scratch_shapes=[pltpu.VMEM(shape, dtype) for shape, dtype in scratch]
        + [
            pltpu.SemaphoreType.DMA((N_SEM,)),
            pltpu.SemaphoreType.DMA((N_SEM,)),
            pltpu.SemaphoreType.DMA((N_LOCAL,)),
        ],
        compiler_params=pltpu.CompilerParams(
            collective_id=0, has_side_effects=True, vmem_limit_bytes=60 * 2**20
        ),
        cost_estimate=pl.CostEstimate(
            flops=5_000_000_000, bytes_accessed=8_000_000, transcendentals=0
        ),
    )(w_value[0], w_out_t[0], layer_input[0], grad_out[0], heads_out[0], probs[0])
    return down[None], above[None], gval[None], gout[None]


def solution(mesh):
    in_specs = (
        P("section", None, "dp", None),
        P("section", None, "dp", None),
        P("section", None, "dp", None),
        P("section", None, "dp", None),
        P("section", "dp", None, None),
        P("section", None, None, "dp", None),
    )
    out_specs = (P("section", "dp", None),) * 4
    return jax.shard_map(
        on_device, mesh=mesh, in_specs=in_specs, out_specs=out_specs, check_vma=False
    )
```

```python
import itertools

import jax
import jax.numpy as jnp
from jax import lax
from jax.experimental import pallas as pl
from jax.experimental.pallas import tpu as pltpu
from jax.sharding import PartitionSpec as P

F = 144
T = 2048
H = 1024
SEQ = 128
HD = 128
HALF = 512
BF = jnp.bfloat16
F32 = jnp.float32
N_SEM = 136
N_LOCAL = 20


def contract(a, b, da, db):
    return lax.dot_general(a, b, (((da,), (db,)), ((), ())), preferred_element_type=F32)


def kernel(
    w_v, w_o, x_in, g_in, hd_in, pr_in,
    ndn, nup, gval, gout,
    raw, hc, gall, goth, wall, hd, sp, own, r1, r2, pb, vall, xb, wvb, vacc, pacc, pbf,
    oacc, obk, orx, ofin, mo_s, mo_r, lo_r, mv_s, mv_r, lv_r, fin_o, fin_v, zero,
    ssem, rsem, lsem,
):
    sec = lax.axis_index("section")
    dp = lax.axis_index("dp")
    xh = dp // 8
    y = (dp // 2) % 4
    k = dp % 2
    o = 1 - k
    xo = 1 - xh
    yp, y2, ym = (y + 1) % 4, (y + 2) % 4, (y + 3) % 4
    around = (y, yp, y2, ym)

    def dev(a, b, c):
        return {"dp": a * 8 + b * 2 + c}

    sib, par, pao = dev(xh, y, o), dev(xo, y, k), dev(xo, y, o)
    up, dn = dev(xh, yp, k), dev(xh, ym, k)
    has_above = sec < 15
    has_below = sec > 0
    is0 = k == 0
    is1 = k == 1
    halo_ok = jnp.logical_or(jnp.logical_and(is0, has_below), jnp.logical_and(is1, has_above))
    halo_sec = jnp.clip(sec - 1 + 2 * k, 0, 15)

    counter = itertools.count()
    locals_ = itertools.count()
    sent = []

    def alloc(n=1):
        first = next(counter)
        for _ in range(n - 1):
            next(counter)
        assert first + n <= N_SEM
        return first

    def remote(src, dst, to, n, m=None):
        return pltpu.make_async_remote_copy(
            src_ref=src, dst_ref=dst, send_sem=ssem.at[n], recv_sem=rsem.at[n if m is None else m],
            device_id=to, device_id_type=pl.DeviceIdType.MESH,
        )

    def push(src, dst, to, n=None):
        copy = remote(src, dst, to, alloc() if n is None else n)
        copy.start()
        sent.append(copy)
        return copy

    def arrive(dst, n):
        remote(dst, dst, sib, n).wait_recv()

    def pull(src, dst):
        copy = pltpu.make_async_copy(src, dst, lsem.at[next(locals_)])
        copy.start()
        return copy

    tcol = xh * 1024
    ocol = xo * 1024

    def cols(base, yy, width=256):
        return pl.ds(pl.multiple_of(base + yy * 256, 256), width)

    own_hd = pull(hd_in, raw)
    own_w = [
        pull(w_o.at[k, :, pl.ds(h * HALF, HALF)], wall.at[h, k]) for h in range(2)
    ]
    own_g = [pull(g_in.at[k, :, cols(tcol, yy)], gall.at[yy, k]) for yy in range(4)]
    own_rest = [
        pull(pr_in.at[k], pb.at[k]),
        pull(w_v.at[k], wvb.at[k]),
        pull(x_in.at[k], xb.at[k]),
        pull(g_in.at[k, :, cols(ocol, 0, 1024)], goth.at[k]),
    ]

    barrier = pltpu.get_barrier_semaphore()

    def greet(to):
        pl.semaphore_signal(barrier, inc=1, device_id=to, device_id_type=pl.DeviceIdType.MESH)

    for to in (sib, par, pao, up, dn):
        greet(to)
    greet({"section": 15 - sec, "dp": xh * 8 + y * 2 + 1})

    @pl.when(has_above)
    def _():
        greet({"section": jnp.minimum(sec + 1, 15), "dp": xh * 8 + y * 2})

    @pl.when(has_below)
    def _():
        greet({"section": jnp.maximum(sec - 1, 0), "dp": xh * 8 + y * 2 + 1})

    own_hd.wait()
    for c in range(2):
        hc[c] = raw[:, c, :]
    hd[y, k] = hc[k]
    pl.semaphore_wait(barrier, 5 + 2 * k + 2 * halo_ok.astype(jnp.int32))

    h_up, h_dn = alloc(2), alloc(2)
    hd_sib = push(hc.at[o], hd.at[y, k], sib)
    push(hc.at[k], hd.at[y, k], up, h_up + k)
    push(hc.at[k], hd.at[y, k], dn, h_dn + k)
    w_copies = {}

    def send_w(h):
        part = pl.ds(h * HALF, HALF)
        w_copies[h] = [
            push(w_o.at[o, :, part], wall.at[h, k], sib),
            push(w_o.at[k, :, part], wall.at[h, 2 + k], par),
            push(w_o.at[o, :, part], wall.at[h, 2 + k], pao),
        ]

    g_copies = {}

    def send_g(d):
        yy = around[d]
        g_copies[d] = [
            push(g_in.at[o, :, cols(tcol, yy)], gall.at[yy, k], sib),
            push(g_in.at[k, :, cols(ocol, yy)], gall.at[yy, 2 + k], par),
            push(g_in.at[o, :, cols(ocol, yy)], gall.at[yy, 2 + k], pao),
        ]

    send_w(0)
    for d in (2, 1, 3):
        send_g(d)
    send_w(1)
    send_g(0)

    hd_sib.wait_recv()
    push(hd.at[y, o], hd.at[y, o], up, h_up + o)
    push(hd.at[y, o], hd.at[y, o], dn, h_dn + o)
    rest = [
        push(pr_in.at[o], pb.at[k], sib),
        push(w_v.at[o], wvb.at[k], sib),
        push(x_in.at[o], xb.at[k], sib),
        push(g_in.at[o, :, cols(ocol, 0, 1024)], goth.at[k], sib),
    ]

    zero[...] = jnp.zeros_like(zero)
    zero_sem = next(locals_)

    @pl.when(jnp.logical_not(has_above))
    def _():
        pltpu.make_async_copy(zero, ndn, lsem.at[zero_sem]).start()

    @pl.when(jnp.logical_not(has_below))
    def _():
        pltpu.make_async_copy(zero, nup, lsem.at[zero_sem]).start()

    arrive(hd.at[ym, 0], h_up)
    hd_f_up = push(hd.at[ym, 0], hd.at[ym, 0], up)
    arrive(hd.at[yp, 1], h_dn + 1)
    hd_f_dn = push(hd.at[yp, 1], hd.at[yp, 1], dn)

    for copy in own_w + own_g:
        copy.wait()

    def weights(h):
        for copy in w_copies[h]:
            copy.wait_recv()

    def partial(d, h):
        if h == 0:
            for copy in g_copies[d]:
                copy.wait_recv()
        part = contract(
            gall[around[d]].reshape(4 * F, 256), wall[h].reshape(4 * F, HALF), 0, 0
        )
        for q in range(2):
            piece = part[q * SEQ : (q + 1) * SEQ]
            if d == 0:
                own[h, q] = piece
            else:
                sp[d, h, q] = piece.astype(BF)

    def out_term(d, first=False):
        term = contract(
            gall[around[d]].reshape(4 * F, 256), hd[around[d]].reshape(256, H), 1, 0
        )
        for h in range(2):
            half = term[:, h * HALF : (h + 1) * HALF].reshape(4, F, HALF)
            if first:
                oacc[h] = half
            else:
                oacc[h] += half

    s1 = {}
    s2 = {}

    def ring_first(h):
        s1[h] = [
            push(sp.at[2, h, 0], r1.at[0, h], up),
            push(sp.at[2, h, 1], r1.at[1, h], dn),
        ]

    def ring_up(h):
        s2[h, 0] = push(sp.at[1, h, 1], r2.at[0, h, 1], up)

    def ring_dn(h):
        s2[h, 1] = push(sp.at[3, h, 0], r2.at[1, h, 0], dn)

    def ring_sum(h):
        s1[h][0].wait_recv()
        sp[1, h, 0] = (sp[1, h, 0].astype(F32) + r1[0, h].astype(F32)).astype(BF)
        s2[h, 2] = push(sp.at[1, h, 0], r2.at[0, h, 0], up)
        s1[h][1].wait_recv()
        sp[3, h, 1] = (sp[3, h, 1].astype(F32) + r1[1, h].astype(F32)).astype(BF)
        s2[h, 3] = push(sp.at[3, h, 1], r2.at[1, h, 1], dn)

    def ring(h):
        weights(h)
        partial(2, h)
        ring_first(h)
        partial(1, h)
        ring_up(h)
        partial(3, h)
        ring_dn(h)

    ring(0)
    ring_sum(0)
    arrive(hd.at[yp, 0], h_dn)
    out_term(1, first=True)
    arrive(hd.at[ym, 1], h_up + 1)
    out_term(3)
    ring(1)
    hd_f_up.wait_recv()
    hd_f_dn.wait_recv()
    out_term(2)
    partial(0, 0)
    out_term(0)
    for h in range(2):
        obk[h] = oacc[h, 2:4].astype(BF)
    out_back = [push(obk.at[0], orx.at[0], par)]
    ring_sum(1)
    partial(0, 1)

    for copy in own_rest:
        copy.wait()
    for copy in rest:
        copy.wait_recv()

    v_sent = {}

    def attention(h):
        for i in range(4):
            s2[h, i].wait_recv()
        for q in range(2):
            total = own[h, q] + r2[0, h, q].astype(F32) + r2[1, h, q].astype(F32)
            total = total.astype(BF)
            for e in range(4):
                vall[h, xh, y, q, :, e * HD : (e + 1) * HD] = contract(
                    pb[q, h * 4 + e], total[:, e * HD : (e + 1) * HD], 0, 0
                ).astype(BF)
        mine = vall.at[h, xh, y]
        v_sent[h, "x"] = push(mine, mine, par)

    def spread(h, side, late):
        mine = vall.at[h, (xh, xo)[side], y]
        for q, way, to in ((late, "u", up), (1 - late, "d", dn)):
            v_sent[h, side, way, q] = push(mine.at[q], mine.at[q], to)

    def spread_own(h, late):
        spread(h, 0, late)

    def spread_other(h):
        v_sent[h, "x"].wait_recv()
        spread(h, 1, 0)
        spread(h, 1, 1)

    def forward(h, side):
        xx = (xh, xo)[side]
        v_sent[h, side, "u", 0].wait_recv()
        piece = vall.at[h, xx, ym, 0]
        v_sent[h, side, "fu"] = push(piece, piece, up)
        v_sent[h, side, "d", 1].wait_recv()
        piece = vall.at[h, xx, yp, 1]
        v_sent[h, side, "fd"] = push(piece, piece, dn)

    def near(h, side):
        v_sent[h, side, "u", 1].wait_recv()
        v_sent[h, side, "d", 0].wait_recv()

    def far(h, side):
        v_sent[h, side, "fu"].wait_recv()
        v_sent[h, side, "fd"].wait_recv()

    halo_sem = alloc(16)
    halo_send = alloc(16)
    halos = []

    def use(h, side, d, first=False):
        xx, yy = (xh, xo)[side], around[d]
        at = cols(xx * 1024, yy)
        block = vall[h, xx, yy].reshape(256, HALF)
        term = contract(xb[:, :, at].reshape(2 * F, 256), block, 1, 0).reshape(2, F, HALF)
        if first:
            vacc[h] = term
        else:
            vacc[h] += term
        back = contract(
            wvb[:, :, h * HALF : (h + 1) * HALF].reshape(2 * F, HALF), block, 1, 1
        )
        i = side * 4 + d
        if h == 0:
            pacc[i] = back
            return
        g_here = gall[yy, 0:2] if side == 0 else goth[:, :, cols(0, yy)]
        total = g_here.reshape(2 * F, 256).astype(F32) + (pacc[i] + back)
        pbf[i] = total.astype(BF).reshape(2, F, 256)
        for core, there, out in ((is0, has_below, ndn), (is1, has_above, nup)):
            copies = [
                remote(
                    pbf.at[i, b], out.at[:, at],
                    {"section": halo_sec, "dp": xh * 8 + y * 2 + b},
                    halo_send + 2 * i + b, halo_sem + 8 * k + i,
                )
                for b in range(2)
            ]

            @pl.when(jnp.logical_and(core, there))
            def _(copies=copies):
                for copy in copies:
                    copy.start()

        halos.extend(copies)

    mirror = [{"section": 15 - sec, "dp": xh * 8 + y * 2 + b} for b in range(2)]
    m_out, m_val = [alloc(2), alloc(2)], [alloc(2), alloc(2)]
    l_out, l_val = [alloc(), alloc()], [alloc(), alloc()]
    mirrors = []
    handed = []

    def share(result, send, land, land_core, n_mirror, n_core):
        copies = [remote(send.at[b], land, mirror[b], n_mirror + b, n_mirror) for b in range(2)]
        mirrors.extend(copies)
        over = remote(result.at[1], land_core, sib, n_core)
        handed.append(over)

        @pl.when(is1)
        def _():
            send[...] = result[...].astype(BF)
            for copy in copies:
                copy.start()

        @pl.when(is0)
        def _():
            over.start()

    stores = []

    def settle(result, land, land_core, n_mirror, n_core, total, target):
        @pl.when(is0)
        def _():
            land_core[...] = result[0]

        @pl.when(is1)
        def _():
            arrive(land_core, n_core)

        arrive(land, n_mirror)
        total[...] = land_core[...] + land[...].astype(F32)
        stores.append(pull(total, target))

    def share_out(h):
        out_back[h].wait_recv()
        ofin[h] = oacc[h, 0:2] + orx[h].astype(F32)
        share(ofin.at[h], mo_s.at[h], mo_r.at[h], lo_r.at[h], m_out[h], l_out[h])

    def share_value(h):
        share(vacc.at[h], mv_s.at[h], mv_r.at[h], lv_r.at[h], m_val[h], l_val[h])

    def settle_out(h):
        settle(
            ofin.at[h], mo_r.at[h], lo_r.at[h], m_out[h], l_out[h],
            fin_o.at[h], gout.at[:, pl.ds(h * HALF, HALF)],
        )

    def settle_value(h):
        settle(
            vacc.at[h], mv_r.at[h], lv_r.at[h], m_val[h], l_val[h],
            fin_v.at[h], gval.at[:, pl.ds(h * HALF, HALF)],
        )

    attention(0)
    spread_own(0, 0)
    spread_own(0, 1)
    out_back.append(push(obk.at[1], orx.at[1], par))
    attention(1)
    spread_other(0)
    forward(0, 0)
    share_out(0)
    use(0, 0, 0, first=True)
    use(1, 0, 0, first=True)
    spread_own(1, 0)
    use(0, 1, 0)
    near(0, 0)
    use(0, 0, 1)
    use(0, 0, 3)
    forward(0, 1)
    spread_own(1, 1)
    spread_other(1)
    share_out(1)
    use(1, 1, 0)
    far(0, 0)
    use(0, 0, 2)
    near(0, 1)
    use(0, 1, 1)
    use(0, 1, 3)
    far(0, 1)
    use(0, 1, 2)
    share_value(0)
    forward(1, 0)
    near(1, 0)
    use(1, 0, 1)
    use(1, 0, 3)
    settle_out(0)
    forward(1, 1)
    far(1, 0)
    use(1, 0, 2)
    settle_out(1)
    near(1, 1)
    use(1, 1, 1)
    use(1, 1, 3)
    far(1, 1)
    use(1, 1, 2)
    share_value(1)
    settle_value(0)

    for copy in sent:
        copy.wait_send()

    @pl.when(halo_ok)
    def _():
        for copy in halos:
            copy.wait_send()

    @pl.when(jnp.logical_not(jnp.logical_and(has_above, has_below)))
    def _():
        pltpu.make_async_copy(zero, ndn, lsem.at[zero_sem]).wait()

    for core, there, out in ((0, has_above, ndn), (1, has_below, nup)):

        @pl.when(there)
        def _(core=core, out=out):
            for i in range(8):
                arrive(out.at[:, pl.ds(i * 256, 256)], halo_sem + 8 * core + i)

    settle_value(1)

    @pl.when(is1)
    def _():
        for copy in mirrors:
            copy.wait_send()

    @pl.when(is0)
    def _():
        for copy in handed:
            copy.wait_send()

    for copy in stores:
        copy.wait()


def hand_over(*refs):
    inputs, outputs, held, sems = refs[:4], refs[4:8], refs[8:12], refs[12]
    reads = [pltpu.make_async_copy(inputs[i], held[i], sems.at[i]) for i in range(4)]
    writes = [pltpu.make_async_copy(held[i], outputs[i], sems.at[4 + i]) for i in range(4)]
    for copy in reads:
        copy.start()
    for read, write in zip(reads, writes):
        read.wait()
        write.start()
    for copy in writes:
        copy.wait()


def on_device(w_value, w_out_t, layer_input, grad_out, heads_out, probs):
    any_ = pl.BlockSpec(memory_space=pl.ANY)
    scratch = [
        ((SEQ, 2, H), BF),
        ((2, SEQ, H), BF),
        ((4, 4, F, 256), BF),
        ((2, F, 1024), BF),
        ((2, 4, F, HALF), BF),
        ((4, 2, SEQ, H), BF),
        ((4, 2, 2, SEQ, HALF), BF),
        ((2, 2, SEQ, HALF), F32),
        ((2, 2, SEQ, HALF), BF),
        ((2, 2, 2, SEQ, HALF), BF),
        ((2, 8, SEQ, SEQ), BF),
        ((2, 2, 4, 2, SEQ, HALF), BF),
        ((2, F, T), BF),
        ((2, F, H), BF),
        ((2, 2, F, HALF), F32),
        ((8, 2 * F, 256), F32),
        ((8, 2, F, 256), BF),
        ((2, 4, F, HALF), F32),
        ((2, 2, F, HALF), BF),
        ((2, 2, F, HALF), BF),
        ((2, 2, F, HALF), F32),
        ((2, 2, F, HALF), BF),
        ((2, F, HALF), BF),
        ((2, F, HALF), F32),
        ((2, 2, F, HALF), BF),
        ((2, F, HALF), BF),
        ((2, F, HALF), F32),
        ((2, F, HALF), F32),
        ((2, F, HALF), F32),
        ((F, T), BF),
    ]
    down, above, gval, gout = pl.pallas_call(
        kernel,
        out_shape=(
            jax.ShapeDtypeStruct((F, T), BF),
            jax.ShapeDtypeStruct((F, T), BF),
            jax.ShapeDtypeStruct((F, H), F32),
            jax.ShapeDtypeStruct((F, H), F32),
        ),
        in_specs=[any_] * 6,
        out_specs=(any_,) * 4,
        scratch_shapes=[pltpu.VMEM(shape, dtype) for shape, dtype in scratch]
        + [
            pltpu.SemaphoreType.DMA((N_SEM,)),
            pltpu.SemaphoreType.DMA((N_SEM,)),
            pltpu.SemaphoreType.DMA((N_LOCAL,)),
        ],
        compiler_params=pltpu.CompilerParams(
            collective_id=0, has_side_effects=True, vmem_limit_bytes=60 * 2**20
        ),
        cost_estimate=pl.CostEstimate(
            flops=5_000_000_000, bytes_accessed=8_000_000, transcendentals=0
        ),
    )(w_value[0], w_out_t[0], layer_input[0], grad_out[0], heads_out[0], probs[0])
    shapes = tuple(
        jax.ShapeDtypeStruct(a.shape, a.dtype) for a in (down, above, gval, gout)
    )
    results = pl.pallas_call(
        hand_over,
        out_shape=shapes,
        in_specs=[any_] * 4,
        out_specs=(any_,) * 4,
        scratch_shapes=[pltpu.VMEM(a.shape, a.dtype) for a in shapes]
        + [pltpu.SemaphoreType.DMA((8,))],
    )(down, above, gval, gout)
    return tuple(a[None] for a in results)


def solution(mesh):
    in_specs = (
        P("section", None, "dp", None),
        P("section", None, "dp", None),
        P("section", None, "dp", None),
        P("section", None, "dp", None),
        P("section", "dp", None, None),
        P("section", None, None, "dp", None),
    )
    out_specs = (P("section", "dp", None),) * 4
    return jax.shard_map(
        on_device, mesh=mesh, in_specs=in_specs, out_specs=out_specs, check_vma=False
    )
```

```python
import itertools

import jax
import jax.numpy as jnp
from jax import lax
from jax.experimental import pallas as pl
from jax.experimental.pallas import tpu as pltpu
from jax.sharding import PartitionSpec as P

F = 144
T = 2048
H = 1024
SEQ = 128
HD = 128
HALF = 512
BF = jnp.bfloat16
F32 = jnp.float32
N_SEM = 136
N_LOCAL = 20


def contract(a, b, da, db):
    return lax.dot_general(a, b, (((da,), (db,)), ((), ())), preferred_element_type=F32)


def kernel(
    w_v, w_o, x_in, g_in, hd_in, pr_in,
    ndn, nup, gval, gout,
    raw, hc, gall, goth, wall, hd, sp, own, r1, r2, pb, vall, xb, wvb, vacc, pacc, pbf,
    oacc, obk, orx, ofin, mo_s, mo_r, lo_r, mv_s, mv_r, lv_r, fin_o, fin_v, zero,
    ssem, rsem, lsem,
):
    sec = lax.axis_index("section")
    dp = lax.axis_index("dp")
    xh = dp // 8
    y = (dp // 2) % 4
    k = dp % 2
    o = 1 - k
    xo = 1 - xh
    yp, y2, ym = (y + 1) % 4, (y + 2) % 4, (y + 3) % 4
    around = (y, yp, y2, ym)

    def dev(a, b, c):
        return {"dp": a * 8 + b * 2 + c}

    sib, par, pao = dev(xh, y, o), dev(xo, y, k), dev(xo, y, o)
    up, dn = dev(xh, yp, k), dev(xh, ym, k)
    has_above = sec < 15
    has_below = sec > 0
    is0 = k == 0
    is1 = k == 1
    halo_ok = jnp.logical_or(jnp.logical_and(is0, has_below), jnp.logical_and(is1, has_above))
    halo_sec = jnp.clip(sec - 1 + 2 * k, 0, 15)

    counter = itertools.count()
    locals_ = itertools.count()
    sent = []

    def alloc(n=1):
        first = next(counter)
        for _ in range(n - 1):
            next(counter)
        assert first + n <= N_SEM
        return first

    def remote(src, dst, to, n, m=None):
        return pltpu.make_async_remote_copy(
            src_ref=src, dst_ref=dst, send_sem=ssem.at[n], recv_sem=rsem.at[n if m is None else m],
            device_id=to, device_id_type=pl.DeviceIdType.MESH,
        )

    def push(src, dst, to, n=None):
        copy = remote(src, dst, to, alloc() if n is None else n)
        copy.start()
        sent.append(copy)
        return copy

    def arrive(dst, n):
        remote(dst, dst, sib, n).wait_recv()

    def pull(src, dst):
        copy = pltpu.make_async_copy(src, dst, lsem.at[next(locals_)])
        copy.start()
        return copy

    tcol = xh * 1024
    ocol = xo * 1024

    def cols(base, yy, width=256):
        return pl.ds(pl.multiple_of(base + yy * 256, 256), width)

    own_hd = pull(hd_in, raw)
    own_w = [
        pull(w_o.at[k, :, pl.ds(h * HALF, HALF)], wall.at[h, k]) for h in range(2)
    ]
    own_g = [pull(g_in.at[k, :, cols(tcol, yy)], gall.at[yy, k]) for yy in range(4)]
    own_rest = [
        pull(pr_in.at[k], pb.at[k]),
        pull(w_v.at[k], wvb.at[k]),
        pull(x_in.at[k], xb.at[k]),
        pull(g_in.at[k, :, cols(ocol, 0, 1024)], goth.at[k]),
    ]

    barrier = pltpu.get_barrier_semaphore()

    def greet(to):
        pl.semaphore_signal(barrier, inc=1, device_id=to, device_id_type=pl.DeviceIdType.MESH)

    for to in (sib, par, pao, up, dn):
        greet(to)
    greet({"section": 15 - sec, "dp": dp})

    @pl.when(has_above)
    def _():
        greet({"section": jnp.minimum(sec + 1, 15), "dp": xh * 8 + y * 2})

    @pl.when(has_below)
    def _():
        greet({"section": jnp.maximum(sec - 1, 0), "dp": xh * 8 + y * 2 + 1})

    own_hd.wait()
    for c in range(2):
        hc[c] = raw[:, c, :]
    hd[y, k] = hc[k]
    pl.semaphore_wait(barrier, 6 + 2 * halo_ok.astype(jnp.int32))

    h_up, h_dn = alloc(2), alloc(2)
    hd_sib = push(hc.at[o], hd.at[y, k], sib)
    push(hc.at[k], hd.at[y, k], up, h_up + k)
    push(hc.at[k], hd.at[y, k], dn, h_dn + k)
    w_copies = {}

    def send_w(h):
        part = pl.ds(h * HALF, HALF)
        w_copies[h] = [
            push(w_o.at[o, :, part], wall.at[h, k], sib),
            push(w_o.at[k, :, part], wall.at[h, 2 + k], par),
            push(w_o.at[o, :, part], wall.at[h, 2 + k], pao),
        ]

    g_copies = {}

    def send_g(d):
        yy = around[d]
        g_copies[d] = [
            push(g_in.at[o, :, cols(tcol, yy)], gall.at[yy, k], sib),
            push(g_in.at[k, :, cols(ocol, yy)], gall.at[yy, 2 + k], par),
            push(g_in.at[o, :, cols(ocol, yy)], gall.at[yy, 2 + k], pao),
        ]

    send_w(0)
    for d in (2, 1, 3):
        send_g(d)
    send_w(1)
    send_g(0)

    hd_sib.wait_recv()
    push(hd.at[y, o], hd.at[y, o], up, h_up + o)
    push(hd.at[y, o], hd.at[y, o], dn, h_dn + o)
    rest = [
        push(pr_in.at[o], pb.at[k], sib),
        push(w_v.at[o], wvb.at[k], sib),
        push(x_in.at[o], xb.at[k], sib),
        push(g_in.at[o, :, cols(ocol, 0, 1024)], goth.at[k], sib),
    ]

    zero[...] = jnp.zeros_like(zero)
    zero_sem = next(locals_)

    @pl.when(jnp.logical_not(has_above))
    def _():
        pltpu.make_async_copy(zero, ndn, lsem.at[zero_sem]).start()

    @pl.when(jnp.logical_not(has_below))
    def _():
        pltpu.make_async_copy(zero, nup, lsem.at[zero_sem]).start()

    arrive(hd.at[ym, 0], h_up)
    hd_f_up = push(hd.at[ym, 0], hd.at[ym, 0], up)
    arrive(hd.at[yp, 1], h_dn + 1)
    hd_f_dn = push(hd.at[yp, 1], hd.at[yp, 1], dn)

    for copy in own_w + own_g:
        copy.wait()

    def weights(h):
        for copy in w_copies[h]:
            copy.wait_recv()

    def partial(d, h):
        if h == 0:
            for copy in g_copies[d]:
                copy.wait_recv()
        part = contract(
            gall[around[d]].reshape(4 * F, 256), wall[h].reshape(4 * F, HALF), 0, 0
        )
        for q in range(2):
            piece = part[q * SEQ : (q + 1) * SEQ]
            if d == 0:
                own[h, q] = piece
            else:
                sp[d, h, q] = piece.astype(BF)

    def out_term(d, first=False):
        term = contract(
            gall[around[d]].reshape(4 * F, 256), hd[around[d]].reshape(256, H), 1, 0
        )
        for h in range(2):
            half = term[:, h * HALF : (h + 1) * HALF].reshape(4, F, HALF)
            if first:
                oacc[h] = half
            else:
                oacc[h] += half

    s1 = {}
    s2 = {}

    def ring_first(h):
        s1[h] = [
            push(sp.at[2, h, 0], r1.at[0, h], up),
            push(sp.at[2, h, 1], r1.at[1, h], dn),
        ]

    def ring_up(h):
        s2[h, 0] = push(sp.at[1, h, 1], r2.at[0, h, 1], up)

    def ring_dn(h):
        s2[h, 1] = push(sp.at[3, h, 0], r2.at[1, h, 0], dn)

    def ring_sum(h):
        s1[h][0].wait_recv()
        sp[1, h, 0] = (sp[1, h, 0].astype(F32) + r1[0, h].astype(F32)).astype(BF)
        s2[h, 2] = push(sp.at[1, h, 0], r2.at[0, h, 0], up)
        s1[h][1].wait_recv()
        sp[3, h, 1] = (sp[3, h, 1].astype(F32) + r1[1, h].astype(F32)).astype(BF)
        s2[h, 3] = push(sp.at[3, h, 1], r2.at[1, h, 1], dn)

    def ring(h):
        weights(h)
        partial(2, h)
        ring_first(h)
        partial(1, h)
        ring_up(h)
        partial(3, h)
        ring_dn(h)

    ring(0)
    ring_sum(0)
    arrive(hd.at[yp, 0], h_dn)
    out_term(1, first=True)
    arrive(hd.at[ym, 1], h_up + 1)
    out_term(3)
    ring(1)
    hd_f_up.wait_recv()
    hd_f_dn.wait_recv()
    out_term(2)
    partial(0, 0)
    out_term(0)
    for h in range(2):
        obk[h] = oacc[h, 2:4].astype(BF)
    out_back = [push(obk.at[0], orx.at[0], par)]
    ring_sum(1)
    partial(0, 1)

    for copy in own_rest:
        copy.wait()
    for copy in rest:
        copy.wait_recv()

    v_sent = {}

    def attention(h):
        for i in range(4):
            s2[h, i].wait_recv()
        for q in range(2):
            total = own[h, q] + r2[0, h, q].astype(F32) + r2[1, h, q].astype(F32)
            total = total.astype(BF)
            for e in range(4):
                vall[h, xh, y, q, :, e * HD : (e + 1) * HD] = contract(
                    pb[q, h * 4 + e], total[:, e * HD : (e + 1) * HD], 0, 0
                ).astype(BF)
        mine = vall.at[h, xh, y]
        v_sent[h, "x"] = push(mine, mine, par)

    def spread(h, side, late):
        mine = vall.at[h, (xh, xo)[side], y]
        for q, way, to in ((late, "u", up), (1 - late, "d", dn)):
            v_sent[h, side, way, q] = push(mine.at[q], mine.at[q], to)

    def spread_own(h, late):
        spread(h, 0, late)

    def spread_other(h):
        v_sent[h, "x"].wait_recv()
        spread(h, 1, 0)
        spread(h, 1, 1)

    def forward(h, side):
        xx = (xh, xo)[side]
        v_sent[h, side, "u", 0].wait_recv()
        piece = vall.at[h, xx, ym, 0]
        v_sent[h, side, "fu"] = push(piece, piece, up)
        v_sent[h, side, "d", 1].wait_recv()
        piece = vall.at[h, xx, yp, 1]
        v_sent[h, side, "fd"] = push(piece, piece, dn)

    def near(h, side):
        v_sent[h, side, "u", 1].wait_recv()
        v_sent[h, side, "d", 0].wait_recv()

    def far(h, side):
        v_sent[h, side, "fu"].wait_recv()
        v_sent[h, side, "fd"].wait_recv()

    halo_sem = alloc(16)
    halo_send = alloc(16)
    halos = []

    def use(h, side, d, first=False):
        xx, yy = (xh, xo)[side], around[d]
        at = cols(xx * 1024, yy)
        block = vall[h, xx, yy].reshape(256, HALF)
        term = contract(xb[:, :, at].reshape(2 * F, 256), block, 1, 0).reshape(2, F, HALF)
        if first:
            vacc[h] = term
        else:
            vacc[h] += term
        back = contract(
            wvb[:, :, h * HALF : (h + 1) * HALF].reshape(2 * F, HALF), block, 1, 1
        )
        i = side * 4 + d
        if h == 0:
            pacc[i] = back
            return
        g_here = gall[yy, 0:2] if side == 0 else goth[:, :, cols(0, yy)]
        total = g_here.reshape(2 * F, 256).astype(F32) + (pacc[i] + back)
        pbf[i] = total.astype(BF).reshape(2, F, 256)
        for core, there, out in ((is0, has_below, ndn), (is1, has_above, nup)):
            copies = [
                remote(
                    pbf.at[i, b], out.at[:, at],
                    {"section": halo_sec, "dp": xh * 8 + y * 2 + b},
                    halo_send + 2 * i + b, halo_sem + 8 * k + i,
                )
                for b in range(2)
            ]

            @pl.when(jnp.logical_and(core, there))
            def _(copies=copies):
                for copy in copies:
                    copy.start()

        halos.extend(copies)

    mirror = {"section": 15 - sec, "dp": dp}
    m_out, m_val = [alloc(2), alloc(2)], [alloc(2), alloc(2)]
    l_out, l_val = [alloc(), alloc()], [alloc(), alloc()]
    mirrors = []
    handed = []
    handed_1 = []

    def share(result, send, land, land_core, n_mirror, n_core):
        mirrors.append(remote(send.at[1], land, mirror, n_mirror))
        between = remote(send.at[0], send.at[1], sib, n_mirror + 1)
        handed_1.append(between)
        over = remote(result.at[1], land_core, sib, n_core)
        handed.append(over)

        @pl.when(is1)
        def _(across=mirrors[-1]):
            send[...] = result[...].astype(BF)
            between.start()
            across.start()

        @pl.when(is0)
        def _():
            over.start()

    def pass_on(send, land, n_mirror):
        @pl.when(is0)
        def _():
            arrive(send.at[1], n_mirror + 1)
            remote(send.at[1], land, mirror, n_mirror).start()

    stores = []

    def settle(result, land, land_core, n_mirror, n_core, total, target):
        @pl.when(is0)
        def _():
            land_core[...] = result[0]

        @pl.when(is1)
        def _():
            arrive(land_core, n_core)

        arrive(land, n_mirror)
        total[...] = land_core[...] + land[...].astype(F32)
        stores.append(pull(total, target))

    def share_out(h):
        out_back[h].wait_recv()
        ofin[h] = oacc[h, 0:2] + orx[h].astype(F32)
        share(ofin.at[h], mo_s.at[h], mo_r.at[h], lo_r.at[h], m_out[h], l_out[h])

    def share_value(h):
        share(vacc.at[h], mv_s.at[h], mv_r.at[h], lv_r.at[h], m_val[h], l_val[h])

    def pass_out(h):
        pass_on(mo_s.at[h], mo_r.at[h], m_out[h])

    def pass_value(h):
        pass_on(mv_s.at[h], mv_r.at[h], m_val[h])

    def settle_out(h):
        settle(
            ofin.at[h], mo_r.at[h], lo_r.at[h], m_out[h], l_out[h],
            fin_o.at[h], gout.at[:, pl.ds(h * HALF, HALF)],
        )

    def settle_value(h):
        settle(
            vacc.at[h], mv_r.at[h], lv_r.at[h], m_val[h], l_val[h],
            fin_v.at[h], gval.at[:, pl.ds(h * HALF, HALF)],
        )

    attention(0)
    spread_own(0, 0)
    spread_own(0, 1)
    out_back.append(push(obk.at[1], orx.at[1], par))
    attention(1)
    spread_other(0)
    forward(0, 0)
    share_out(0)
    use(0, 0, 0, first=True)
    use(1, 0, 0, first=True)
    pass_out(0)
    spread_own(1, 0)
    use(0, 1, 0)
    near(0, 0)
    use(0, 0, 1)
    use(0, 0, 3)
    forward(0, 1)
    spread_own(1, 1)
    spread_other(1)
    share_out(1)
    use(1, 1, 0)
    pass_out(1)
    far(0, 0)
    use(0, 0, 2)
    near(0, 1)
    use(0, 1, 1)
    use(0, 1, 3)
    far(0, 1)
    use(0, 1, 2)
    share_value(0)
    forward(1, 0)
    near(1, 0)
    pass_value(0)
    use(1, 0, 1)
    use(1, 0, 3)
    settle_out(0)
    forward(1, 1)
    far(1, 0)
    use(1, 0, 2)
    settle_out(1)
    near(1, 1)
    use(1, 1, 1)
    use(1, 1, 3)
    far(1, 1)
    use(1, 1, 2)
    share_value(1)
    pass_value(1)
    settle_value(0)

    for copy in sent:
        copy.wait_send()

    @pl.when(halo_ok)
    def _():
        for copy in halos:
            copy.wait_send()

    @pl.when(jnp.logical_not(jnp.logical_and(has_above, has_below)))
    def _():
        pltpu.make_async_copy(zero, ndn, lsem.at[zero_sem]).wait()

    for core, there, out in ((0, has_above, ndn), (1, has_below, nup)):

        @pl.when(there)
        def _(core=core, out=out):
            for i in range(8):
                arrive(out.at[:, pl.ds(i * 256, 256)], halo_sem + 8 * core + i)

    settle_value(1)

    for copy in mirrors:
        copy.wait_send()

    @pl.when(is1)
    def _():
        for copy in handed_1:
            copy.wait_send()

    @pl.when(is0)
    def _():
        for copy in handed:
            copy.wait_send()

    for copy in stores:
        copy.wait()


def hand_over(*refs):
    inputs, outputs, held, sems = refs[:4], refs[4:8], refs[8:12], refs[12]
    reads = [pltpu.make_async_copy(inputs[i], held[i], sems.at[i]) for i in range(4)]
    writes = [pltpu.make_async_copy(held[i], outputs[i], sems.at[4 + i]) for i in range(4)]
    for copy in reads:
        copy.start()
    for read, write in zip(reads, writes):
        read.wait()
        write.start()
    for copy in writes:
        copy.wait()


def on_device(w_value, w_out_t, layer_input, grad_out, heads_out, probs):
    any_ = pl.BlockSpec(memory_space=pl.ANY)
    scratch = [
        ((SEQ, 2, H), BF),
        ((2, SEQ, H), BF),
        ((4, 4, F, 256), BF),
        ((2, F, 1024), BF),
        ((2, 4, F, HALF), BF),
        ((4, 2, SEQ, H), BF),
        ((4, 2, 2, SEQ, HALF), BF),
        ((2, 2, SEQ, HALF), F32),
        ((2, 2, SEQ, HALF), BF),
        ((2, 2, 2, SEQ, HALF), BF),
        ((2, 8, SEQ, SEQ), BF),
        ((2, 2, 4, 2, SEQ, HALF), BF),
        ((2, F, T), BF),
        ((2, F, H), BF),
        ((2, 2, F, HALF), F32),
        ((8, 2 * F, 256), F32),
        ((8, 2, F, 256), BF),
        ((2, 4, F, HALF), F32),
        ((2, 2, F, HALF), BF),
        ((2, 2, F, HALF), BF),
        ((2, 2, F, HALF), F32),
        ((2, 2, F, HALF), BF),
        ((2, F, HALF), BF),
        ((2, F, HALF), F32),
        ((2, 2, F, HALF), BF),
        ((2, F, HALF), BF),
        ((2, F, HALF), F32),
        ((2, F, HALF), F32),
        ((2, F, HALF), F32),
        ((F, T), BF),
    ]
    down, above, gval, gout = pl.pallas_call(
        kernel,
        out_shape=(
            jax.ShapeDtypeStruct((F, T), BF),
            jax.ShapeDtypeStruct((F, T), BF),
            jax.ShapeDtypeStruct((F, H), F32),
            jax.ShapeDtypeStruct((F, H), F32),
        ),
        in_specs=[any_] * 6,
        out_specs=(any_,) * 4,
        scratch_shapes=[pltpu.VMEM(shape, dtype) for shape, dtype in scratch]
        + [
            pltpu.SemaphoreType.DMA((N_SEM,)),
            pltpu.SemaphoreType.DMA((N_SEM,)),
            pltpu.SemaphoreType.DMA((N_LOCAL,)),
        ],
        compiler_params=pltpu.CompilerParams(
            collective_id=0, has_side_effects=True, vmem_limit_bytes=60 * 2**20
        ),
        cost_estimate=pl.CostEstimate(
            flops=5_000_000_000, bytes_accessed=8_000_000, transcendentals=0
        ),
    )(w_value[0], w_out_t[0], layer_input[0], grad_out[0], heads_out[0], probs[0])
    shapes = tuple(
        jax.ShapeDtypeStruct(a.shape, a.dtype) for a in (down, above, gval, gout)
    )
    results = pl.pallas_call(
        hand_over,
        out_shape=shapes,
        in_specs=[any_] * 4,
        out_specs=(any_,) * 4,
        scratch_shapes=[pltpu.VMEM(a.shape, a.dtype) for a in shapes]
        + [pltpu.SemaphoreType.DMA((8,))],
    )(down, above, gval, gout)
    return tuple(a[None] for a in results)


def solution(mesh):
    in_specs = (
        P("section", None, "dp", None),
        P("section", None, "dp", None),
        P("section", None, "dp", None),
        P("section", None, "dp", None),
        P("section", "dp", None, None),
        P("section", None, None, "dp", None),
    )
    out_specs = (P("section", "dp", None),) * 4
    return jax.shard_map(
        on_device, mesh=mesh, in_specs=in_specs, out_specs=out_specs, check_vma=False
    )
```
